128 devices in a mesh: row: 8 (over y_lo, x), col: 16 (over y_hi, z, core).
Axes of the slice: x: 4, y: 4 (y_hi: 2, y_lo: 2; y = y_hi * 2 + y_lo), z: 4, core: 2. Of those that a mesh axis runs over, the one named last changes fastest.
Arguments:
- row_constraints: bfloat16 [2048, 128, 128], P(('row', 'col')), may hold values from -0.5 to 0.5
- row_block: int32 [2048], P(('row', 'col')), may hold values from 0 to 15
- row_slots: int32 [2048, 2], P(('row', 'col')), may hold values from 0 to 1
- col_constraints: bfloat16 [4096, 128, 128], P(('col', 'row')), may hold values from -0.5 to 0.5
- col_block: int32 [4096], P(('col', 'row')), may hold values from 0 to 15
- col_slots: int32 [4096, 2], P(('col', 'row')), may hold values from 0 to 1
- primal_x: bfloat16 [16, 256, 256], replicated, may hold values from -0.5 to 0.5
- inverse_z: bfloat16 [16, 256, 256], replicated, may hold values from -0.5 to 0.5
Outputs:
- schur_cyclic: float32 [16, 128, 4096], P(None, 'row', 'col')
The draws below stay inside these ranges and needn't reach their ends.
All inputs are finite; a program needn't handle non-finite values.
Results may differ from the reference program's by a relative error of at most 0.0065.
Values may be sent and summed in bfloat16 or wider, within the bound.
A program may use at most 192 MiB of HBM per device.

```python
import math
import jax
import jax.numpy as jnp
from jax import lax

BLK = 128
P_SIZE = 2
S = 256
NB = 16
TB = 16
NIR = 256
NI = 2048
NJ = 4096
N_ROW = 8


def touch_ends(values, key, smallest, high):
    extent = values.shape
    place = [jax.random.randint(jax.random.fold_in(key, axis), (), 0, extent[axis]) for axis in range(len(extent))]
    values = values.at[tuple(place)].set(smallest)
    longest = extent.index(max(extent))
    place[longest] = (place[longest] + 1) % extent[longest]
    return values.at[tuple(place)].set(high)


def block_scale(key, extent, split, low, top_value):
    gain, own = 1.0, jax.random.fold_in(key, 6)
    for dim, parts in split:
        draws = jnp.exp(jax.random.uniform(jax.random.fold_in(own, dim), (parts,), jnp.float32, low / len(split), top_value / len(split)))
        gain = gain * jnp.repeat(draws, extent[dim] // parts).reshape([-1 if axis == dim else 1 for axis in range(len(extent))])
    return gain


def noise(own_key, extent, spread, most, split=(), kind=jnp.bfloat16):
    values = spread * jax.random.normal(own_key, extent, jnp.float32)
    if split:
        values = values * block_scale(own_key, extent, split, -0.22, 0.18)
    return jnp.clip(values, -most, most).astype(kind)


def setup_inputs(seed: int = 0) -> dict:
    key_list = jax.random.split(jax.random.key(seed), 9)
    return {
        "row_constraints": noise(key_list[0], (NI, BLK, BLK), BLK ** -0.5, 0.5, ((0, 128),)),
        "row_block": touch_ends(jax.random.randint(key_list[1], (NI,), 0, NB), jax.random.fold_in(key_list[1], 1), 0, NB - 1).astype(jnp.int32),
        "row_slots": touch_ends(jax.random.randint(key_list[2], (NI, 2), 0, P_SIZE), jax.random.fold_in(key_list[2], 1), 0, P_SIZE - 1).astype(jnp.int32),
        "col_constraints": noise(key_list[3], (NJ, BLK, BLK), BLK ** -0.5, 0.5, ((0, 128),)),
        "col_block": touch_ends(jax.random.randint(key_list[4], (NJ,), 0, NB), jax.random.fold_in(key_list[4], 1), 0, NB - 1).astype(jnp.int32),
        "col_slots": touch_ends(jax.random.randint(key_list[5], (NJ, 2), 0, P_SIZE), jax.random.fold_in(key_list[5], 1), 0, P_SIZE - 1).astype(jnp.int32),
        "primal_x": noise(key_list[6], (NB, S, S), BLK ** -0.5, 0.5),
        "inverse_z": noise(key_list[7], (NB, S, S), BLK ** -0.5, 0.5),
    }


def strips_of(matrices, chosen_block, chosen_slot, block_edge):
    sections = matrices.shape[1] // block_edge
    layout = matrices.reshape(matrices.shape[0], sections, block_edge, sections, block_edge)
    layout = jnp.transpose(layout, (0, 3, 1, 2, 4)).reshape(matrices.shape[0] * sections, sections, block_edge, block_edge)
    return jnp.take(layout, (chosen_block * sections + chosen_slot).astype(jnp.int32), axis=0)


def reference(row_constraints, row_block, row_slots, col_constraints, col_block, col_slots, primal_x, inverse_z):
    strips = strips_of(inverse_z, row_block, row_slots[:, 1], BLK)
    images_rows = jnp.einsum("nrs,nbus->nbru", row_constraints.astype(jnp.float32), strips.astype(jnp.float32)).astype(jnp.bfloat16)
    flat_rows = images_rows.reshape(NI * P_SIZE, BLK * BLK)
    levels = jnp.arange(P_SIZE, dtype=jnp.int32)
    row_onehot = (row_slots[:, 0:1] == levels[None, :]).astype(jnp.float32)
    span = math.gcd(NJ, 512)

    def column_block(start):
        constraints = lax.dynamic_slice_in_dim(col_constraints, start, span, 0)
        blocks = lax.dynamic_slice_in_dim(col_block, start, span, 0)
        slots = lax.dynamic_slice_in_dim(col_slots, start, span, 0)
        col_strips = strips_of(primal_x, blocks, slots[:, 0], BLK)
        images_cols = jnp.einsum("nart,ntu->naru", col_strips.astype(jnp.float32), constraints.astype(jnp.float32)).astype(jnp.bfloat16)
        products = jnp.dot(flat_rows, images_cols.reshape(span * P_SIZE, BLK * BLK).T, preferred_element_type=jnp.float32)
        products = products.reshape(NI, P_SIZE, span, P_SIZE)
        col_onehot = (slots[:, 1:2] == levels[None, :]).astype(jnp.float32)
        values = jnp.einsum("ibja,ia,jb->ij", products, row_onehot, col_onehot)
        matching = row_block[:, None] == blocks[None, :]
        return jnp.where(matching, values, jnp.zeros_like(values))

    starts = (jnp.arange(NJ // span, dtype=jnp.int32) * span).astype(jnp.int32)
    pieces = lax.map(column_block, starts)
    schur = jnp.transpose(pieces, (1, 0, 2)).reshape(NI, NJ)
    return schur.reshape(NIR // TB, N_ROW * TB, NJ)
```

```python
import jax
import jax.numpy as jnp
from jax import lax
from jax.experimental import pallas as pl
from jax.experimental.pallas import tpu as pltpu
from jax.sharding import PartitionSpec as P

TB = 16
BLK = 128
S = 256
FLAT = BLK * BLK
WIDE = FLAT + 128
SLICES = 8
SL = FLAT // SLICES
OWN = 32
MESH = pl.DeviceIdType.MESH
F32 = jnp.float32
BF16 = jnp.bfloat16


def lanes_of(s):
    start = s * SL
    stop = WIDE if s == SLICES - 1 else start + SL
    return start, stop


def kernel(
    rows_in, cols_in, lab_in, x_in, w_in, out,
    rb, cb, lab, lab_s, xs, ws, mb, scr, acc, osend,
    row_send, row_recv, sib_send, sib_recv, col_send, col_recv, lab_send, lab_recv,
    out_send, out_recv, local,
):
    row, col = lax.axis_index("row"), lax.axis_index("col")
    y_lo, x = row // 4, row % 4
    y_hi, z, core = col // 8, (col // 2) % 4, col % 2
    y = y_hi * 2 + y_lo

    def dev(x_, y_, z_, core_):
        return ((y_ % 2) * 4 + x_, (y_ // 2) * 8 + z_ * 2 + core_)

    def yy(y_):
        return (y_ % 2) * 2 + y_ // 2

    yp, ym, y2 = (y + 1) % 4, (y + 3) % 4, (y + 2) % 4
    zp, zm, z2 = (z + 1) % 4, (z + 3) % 4, (z + 2) % 4
    xp, xm, x2 = (x + 1) % 4, (x + 3) % 4, (x + 2) % 4
    sibling = dev(x, y, z, 1 - core)
    dev_y = (dev(x, yp, z, core), dev(x, ym, z, core))
    dev_z = (dev(x, y, zp, core), dev(x, y, zm, core))
    dev_x = (dev(xp, y, z, core), dev(xm, y, z, core))

    barrier = pltpu.get_barrier_semaphore()
    y_other = y_hi * 2 + 1 - y_lo
    y_far = (y_other + 2) % 4
    greet = [dev(x, y_far, z, core), *dev_z, sibling]
    greet += [((row + n) % 8, col) for n in range(1, 8)]
    for d in greet:
        pl.semaphore_signal(barrier, inc=1, device_id=d, device_id_type=MESH)

    loads = [
        pltpu.make_async_copy(rows_in, rb.at[z, core, yy(y)], local.at[0]),
        pltpu.make_async_copy(cols_in, cb.at[x], local.at[1]),
        pltpu.make_async_copy(lab_in, lab.at[x], local.at[2]),
        pltpu.make_async_copy(x_in.at[:, :, pl.ds(0, BLK)], xs.at[0], local.at[3]),
        pltpu.make_async_copy(x_in.at[:, :, pl.ds(BLK, BLK)], xs.at[1], local.at[4]),
        pltpu.make_async_copy(w_in, ws, local.at[5]),
    ]
    for c in loads:
        c.start()
    pl.semaphore_wait(barrier, len(greet))

    def remote(src, dst, send, recv, to):
        return pltpu.make_async_remote_copy(
            src_ref=src, dst_ref=dst, send_sem=send, recv_sem=recv, device_id=to, device_id_type=MESH
        )

    sent = []

    def go(c):
        c.start()
        sent.append(c)
        return c

    def first(s):
        a, b = lanes_of(s)
        to = dev_y if s < 4 else dev_z
        return [
            go(remote(rows_in.at[:, a:b], rb.at[z, core, yy(y), :, a:b], row_send.at[s, n], row_recv.at[s, n], to[n]))
            for n in range(2)
        ]

    def second(s):
        a, b = lanes_of(s)
        mid = a + SL // 2
        to = dev_y if s < 4 else dev_z
        slot = [(z, yy(ym)), (z, yy(yp))] if s < 4 else [(zm, yy(y)), (zp, yy(y))]
        cut = [(a, mid), (mid, b)]
        got = []
        for n in range(2):
            (u, v), (c, d) = slot[n], cut[n]
            ref = rb.at[u, core, v, :, c:d]
            got.append(go(remote(ref, ref, row_send.at[s, 2 + n], row_recv.at[s, 2 + n], to[n])))
        return got

    def group(s, u, part=None):
        a, b = lanes_of(s)
        part = pl.ds(0, 4) if part is None else part
        if s < 4:
            return rb.at[u, core, part, :, a:b]
        return rb.at[part, core, yy(u), :, a:b]

    def third(s):
        to = dev_z if s < 4 else dev_y
        ref = group(s, z if s < 4 else y)
        return [go(remote(ref, ref, row_send.at[s, 4 + n], row_recv.at[s, 4 + n], to[n])) for n in range(2)]

    def fourth(s):
        to = dev_z if s < 4 else dev_y
        src = (zm, zp) if s < 4 else (ym, yp)
        got = []
        for n in range(2):
            ref = group(s, src[n], pl.ds(2 * n, 2))
            got.append(go(remote(ref, ref, row_send.at[s, 6 + n], row_recv.at[s, 6 + n], to[n])))
        return got

    def share(s, m):
        u = ((z, zm, zp, z2) if s < 4 else (y, ym, yp, y2))[m]
        ref = group(s, u)
        return go(remote(ref, ref, sib_send.at[s, m], sib_recv.at[s, m], sibling))

    labels = [
        go(remote(lab_in, lab.at[x], lab_send.at[n], lab_recv.at[n], dev((x + n + 1) % 4, y, z, core)))
        for n in range(3)
    ]
    order = [0, 4, 1, 5, 2, 6, 3, 7]
    w1 = {}
    for s in order:
        w1[s] = first(s)
    half = OWN // 2
    c1 = {}
    for h in range(2):
        for n in range(2):
            part = pl.ds((half * h) if n == 0 else (half * (1 - h)), half)
            c1[h, n] = go(remote(
                cols_in.at[part], cb.at[x, part], col_send.at[2 * h + n], col_recv.at[2 * h + n], dev_x[n]
            ))
    for c in loads:
        c.wait()
    acc[...] = jnp.zeros_like(acc)

    def images(xj, h):
        base = h * half

        def one(jj, carry):
            code = lab_s[xj, 0, xj * OWN + base + jj]
            k, p, q = code >> 2, (code >> 1) & 1, code & 1
            t = jnp.dot(cb[xj, base + jj], ws[k * 2 + q], preferred_element_type=F32).astype(BF16)
            m = jnp.dot(xs[p, k], t, preferred_element_type=F32)
            scr[0, pl.ds(jj, S, stride=half), :] = m[:, :BLK]
            scr[1, pl.ds(jj, S, stride=half), :] = m[:, BLK:]
            return carry

        lax.fori_loop(0, half, one, 0, unroll=4)

        def lay(r, carry):
            for a in range(2):
                for b in range(2):
                    at = pl.multiple_of((a * BLK + r) * half, half)
                    v = scr[b, pl.ds(at, half), :]
                    mb[xj, a * 2 + b, pl.ds(base, half), pl.ds(pl.multiple_of(r * BLK, BLK), BLK)] = v.astype(BF16)
            return carry

        lax.fori_loop(0, BLK, lay, 0, unroll=8)

    pairs = ((x, xm), (xp, x2))

    def contract(s, n):
        lo = s * SL
        left = rb[:, :, :, :, lo:lo + SL].reshape(8 * 64, SL)
        right = jnp.concatenate(
            [mb[xj, :, :, lo:lo + SL].reshape(4 * OWN, SL) for xj in pairs[n]], axis=0
        )
        acc[n] += lax.dot_general(left, right, (((1,), (1,)), ((), ())), preferred_element_type=F32)

    for c in labels:
        c.wait_recv()
    lab_copy = pltpu.make_async_copy(lab, lab_s, local.at[6])
    lab_copy.start()
    lab_copy.wait()

    w2, w3, w4, sh = {}, {}, {}, {}
    for s in order:
        for c in w1[s]:
            c.wait_recv()
        w2[s] = second(s)
    images(x, 0)
    for s in order:
        for c in w2[s]:
            c.wait_recv()
        w3[s] = third(s)
        sh[s, 0] = share(s, 0)
    images(x, 1)
    c2 = []
    for n in range(2):
        c1[0, n].wait_recv()
        part = pl.ds(half * n, half)
        ref = cb.at[(xm, xp)[n], part]
        c2.append(go(remote(ref, ref, col_send.at[4 + n], col_recv.at[4 + n], dev_x[n])))
    images(xm, 0)
    images(xp, 1)
    for s in order:
        for c in w3[s]:
            c.wait_recv()
        w4[s] = fourth(s)
        sh[s, 1] = share(s, 1)
        sh[s, 2] = share(s, 2)
    for n in range(2):
        c1[1, n].wait_recv()
    images(xm, 1)
    images(xp, 0)
    for c in c2:
        c.wait_recv()
    images(x2, 0)
    images(x2, 1)
    for s in order:
        for c in w4[s]:
            c.wait_recv()
        sh[s, 3] = share(s, 3)
        for m in range(4):
            sh[s, m].wait_recv()
        contract(s, 0)
        contract(s, 1)

    code = rb[:, :, :, :, FLAT:WIDE].reshape(8 * 64, 128).astype(F32).astype(jnp.int32)
    lane = lax.broadcasted_iota(jnp.int32, (1, 128), 1) // OWN
    chosen = (code & 3) == lane
    col_code = lab[0, 0:1, :] + lab[1, 0:1, :] + lab[2, 0:1, :] + lab[3, 0:1, :]
    total = jnp.zeros((8 * 64, 128), F32)
    for n in range(2):
        for m in range(2):
            v = jnp.where(chosen, acc[n, :, m * 128:(m + 1) * 128], 0.0)
            v = v + pltpu.roll(v, 64, 1)
            v = v + pltpu.roll(v, 32, 1)
            total = jnp.where(lane == pairs[n][m], v, total)
    total = jnp.where((code >> 2) == (col_code >> 2), total, 0.0)
    osend[...] = total.reshape(8, 2, 2, TB, 128)

    place = pl.ds(pl.multiple_of(y_lo * 128, 128), 128)
    keep = pltpu.make_async_copy(osend.at[row], out.at[:, x, :, :, place], local.at[7])
    keep.start()
    outs = []
    for n in range(1, 8):
        to = (row + n) % 8
        outs.append(go(remote(osend.at[to], out.at[:, x, :, :, place], out_send.at[n - 1], out_recv.at[n - 1], (to, col))))
    for c in outs:
        c.wait_recv()
    keep.wait()
    for c in sent:
        c.wait_send()


def per_device(
    row_constraints, row_block, row_slots, col_constraints, col_block, col_slots, primal_x, inverse_z
):
    n_row, n_col = row_constraints.shape[0], col_constraints.shape[0]
    row_code = (row_block * 4 + row_slots[:, 0] * 2 + row_slots[:, 1]).astype(BF16)
    rows = jnp.concatenate(
        [row_constraints.reshape(n_row, FLAT), jnp.broadcast_to(row_code[:, None], (n_row, 128))], axis=1
    )
    col_code = col_block * 4 + col_slots[:, 0] * 2 + col_slots[:, 1]
    mine = lax.axis_index("row") % 4
    lanes = jnp.arange(128, dtype=jnp.int32)
    placed = jnp.where(lanes // n_col == mine, jnp.tile(col_code, 128 // n_col), 0)
    lab = jnp.broadcast_to(placed[None, :], (8, 128))
    any_spec = pl.BlockSpec(memory_space=pl.ANY)
    dma = pltpu.SemaphoreType.DMA
    out = pl.pallas_call(
        kernel,
        out_shape=jax.ShapeDtypeStruct((2, 4, 2, TB, 256), F32),
        in_specs=[any_spec] * 5,
        out_specs=any_spec,
        scratch_shapes=[
            pltpu.VMEM((4, 2, 4, TB, WIDE), BF16),
            pltpu.VMEM((4, OWN, BLK, BLK), BF16),
            pltpu.VMEM((4, 8, 128), jnp.int32),
            pltpu.SMEM((4, 8, 128), jnp.int32),
            pltpu.VMEM((2, 16, S, BLK), BF16),
            pltpu.VMEM((32, BLK, S), BF16),
            pltpu.VMEM((4, 4, OWN, FLAT), BF16),
            pltpu.VMEM((2, S * OWN // 2, BLK), F32),
            pltpu.VMEM((2, 512, 256), F32),
            pltpu.VMEM((8, 2, 2, TB, 128), F32),
            dma((SLICES, 8)), dma((SLICES, 8)),
            dma((SLICES, 4)), dma((SLICES, 4)),
            dma((6,)), dma((6,)),
            dma((3,)), dma((3,)),
            dma((7,)), dma((7,)),
            dma((8,)),
        ],
        compiler_params=pltpu.CompilerParams(
            collective_id=0, has_side_effects=True, vmem_limit_bytes=58 * 1024 * 1024
        ),
    )(rows, col_constraints, lab, primal_x, inverse_z.reshape(32, BLK, S))
    return out.reshape(16, TB, 256)


def solution(mesh):
    placed = (
        P(("row", "col"), None, None),
        P(("row", "col")),
        P(("row", "col"), None),
        P(("col", "row"), None, None),
        P(("col", "row")),
        P(("col", "row"), None),
        P(),
        P(),
    )
    return jax.shard_map(
        per_device, mesh=mesh, in_specs=placed, out_specs=P(None, "row", "col"), check_vma=False
    )
```

```python
import jax
import jax.numpy as jnp
from jax import lax
from jax.experimental import pallas as pl
from jax.experimental.pallas import tpu as pltpu
from jax.sharding import PartitionSpec as P

TB = 16
BLK = 128
S = 256
FLAT = BLK * BLK
WIDE = FLAT + 128
OWN = 32
HALF = OWN // 2
UNIT = 8
STEP = UNIT * BLK
PARTS = (2, 3, 2, 1)
PITCH = 17
MESH = pl.DeviceIdType.MESH
F32 = jnp.float32
BF16 = jnp.bfloat16


def units_of(s):
    start = (s // 4) * (BLK // UNIT // 2) + sum(PARTS[: s % 4])
    return start, start + PARTS[s % 4]


def lanes_of(s):
    first, last = units_of(s)
    return first * STEP, (WIDE if s == 7 else last * STEP)


def kernel(
    row_block, row_slots, col_block, col_slots, rows_in, cols_in, x_in, w_in, out,
    raw, rb, cb, lab, lab_s, xs, ws, mb, scr, acc, osend,
    row_send, row_recv, sib_send, sib_recv, col_send, col_recv, lab_send, lab_recv,
    out_send, out_recv, local,
):
    row, col = lax.axis_index("row"), lax.axis_index("col")
    y_lo, x = row // 4, row % 4
    y_hi, z, core = col // 8, (col // 2) % 4, col % 2
    y = y_hi * 2 + y_lo

    def dev(x_, y_, z_, core_):
        return ((y_ % 2) * 4 + x_, (y_ // 2) * 8 + z_ * 2 + core_)

    def yy(y_):
        return (y_ % 2) * 2 + y_ // 2

    yp, ym, y2 = (y + 1) % 4, (y + 3) % 4, (y + 2) % 4
    zp, zm, z2 = (z + 1) % 4, (z + 3) % 4, (z + 2) % 4
    xp, xm, x2 = (x + 1) % 4, (x + 3) % 4, (x + 2) % 4
    sibling = dev(x, y, z, 1 - core)
    dev_y = (dev(x, yp, z, core), dev(x, ym, z, core))
    dev_z = (dev(x, y, zp, core), dev(x, y, zm, core))
    dev_x = (dev(xp, y, z, core), dev(xm, y, z, core))

    barrier = pltpu.get_barrier_semaphore()
    y_other = y_hi * 2 + 1 - y_lo
    y_far = (y_other + 2) % 4
    greet = [dev(x, y_far, z, core), *dev_z, sibling]
    greet += [((row + n) % 8, col) for n in range(1, 8)]
    for d in greet:
        pl.semaphore_signal(barrier, inc=1, device_id=d, device_id_type=MESH)

    raw_load = pltpu.make_async_copy(rows_in, raw, local.at[0])
    raw_load.start()
    loads = [
        pltpu.make_async_copy(cols_in, cb.at[x], local.at[1]),
        pltpu.make_async_copy(w_in, ws, local.at[2]),
        pltpu.make_async_copy(x_in.at[:, :, pl.ds(0, BLK)], xs.at[0], local.at[3]),
        pltpu.make_async_copy(x_in.at[:, :, pl.ds(BLK, BLK)], xs.at[1], local.at[4]),
    ]
    for c in loads:
        c.start()

    sub = lax.broadcasted_iota(jnp.int32, (TB, 128), 0)
    mark = jnp.zeros((TB, 128), jnp.int32)
    for i in range(TB):
        mark = jnp.where(sub == i, row_block[i] * 4 + row_slots[0, i] * 2 + row_slots[1, i], mark)
    rb[z, core, yy(y), :, FLAT:WIDE] = mark.astype(F32).astype(BF16)
    lane = lax.broadcasted_iota(jnp.int32, (8, 128), 1) - x * OWN
    mark = jnp.zeros((8, 128), jnp.int32)
    for j in range(OWN):
        mark = jnp.where(lane == j, col_block[j] * 4 + col_slots[0, j] * 2 + col_slots[1, j], mark)
    lab[x] = mark

    raw_load.wait()
    for r in range(0, BLK, TB):
        tile = jnp.swapaxes(raw[:, r:r + TB, :], 0, 1)
        for n in range(TB):
            rb[z, core, yy(y), :, (r + n) * BLK:(r + n + 1) * BLK] = tile[n]
    pl.semaphore_wait(barrier, len(greet))

    def remote(src, dst, send, recv, to):
        return pltpu.make_async_remote_copy(
            src_ref=src, dst_ref=dst, send_sem=send, recv_sem=recv, device_id=to, device_id_type=MESH
        )

    sent = []

    def go(c):
        c.start()
        sent.append(c)
        return c

    def move(s, n, ref, to):
        return go(remote(ref, ref, row_send.at[s, n], row_recv.at[s, n], to))

    def block(s, a, b, cut):
        u, v = (b, a) if s < 4 else (a, b)
        return rb.at[u, core, yy(v), :, cut[0]:cut[1]]

    def axes(s):
        return ((y, ym, yp, y2), (z, zm, zp, z2)) if s < 4 else ((z, zm, zp, z2), (y, ym, yp, y2))

    def ways(s):
        return (dev_y, dev_z) if s < 4 else (dev_z, dev_y)

    def group(s, b, part=pl.ds(0, 4)):
        lo, hi = lanes_of(s)
        return rb.at[b, core, part, :, lo:hi] if s < 4 else rb.at[part, core, yy(b), :, lo:hi]

    w1, w2, w3, w4, sh = {}, {}, {}, {}, {}

    def first(s):
        f, g = axes(s)
        ref = block(s, f[0], g[0], lanes_of(s))
        w1[s] = [move(s, n, ref, ways(s)[0][n]) for n in range(2)]

    def second(s):
        for c in w1[s]:
            c.wait_recv()
        f, g = axes(s)
        lo, hi = lanes_of(s)
        mid = lo + PARTS[s % 4] * STEP // 2
        cut = ((lo, mid), (mid, hi))
        w2[s] = [move(s, 2 + n, block(s, f[1 + n], g[0], cut[n]), ways(s)[0][n]) for n in range(2)]

    def arrived(s):
        for c in w2[s]:
            c.wait_recv()
        share(s, 0)

    def third(s):
        ref = group(s, axes(s)[1][0])
        w3[s] = [move(s, 4 + n, ref, ways(s)[1][n]) for n in range(2)]

    def fourth(s):
        for c in w3[s]:
            c.wait_recv()
        f, g = axes(s)
        w4[s] = [move(s, 6 + n, group(s, g[1 + n], pl.ds(2 * n, 2)), ways(s)[1][n]) for n in range(2)]
        share(s, 1)
        share(s, 2)

    def last(s):
        for c in w4[s]:
            c.wait_recv()
        share(s, 3)

    def share(s, m):
        ref = group(s, axes(s)[1][m])
        sh[s, m] = go(remote(ref, ref, sib_send.at[s, m], sib_recv.at[s, m], sibling))

    c1 = {}

    def columns(h):
        for n in range(2):
            part = pl.ds((HALF * h) if n == 0 else (HALF * (1 - h)), HALF)
            c1[h, n] = go(remote(cols_in.at[part], cb.at[x, part], col_send.at[2 * h + n], col_recv.at[2 * h + n], dev_x[n]))

    def columns_far():
        for n in range(2):
            ref = cb.at[(xm, xp)[n], pl.ds(HALF * n, HALF)]
            c1[2, n] = go(remote(ref, ref, col_send.at[4 + n], col_recv.at[4 + n], dev_x[n]))

    def columns_wait(h):
        for n in range(2):
            c1[h, n].wait_recv()

    def images(xj, h, code_of):
        base = h * HALF
        batch = 8

        def some(i, carry):
            js = [i * batch + n for n in range(batch)]
            codes = [code_of(base + j) for j in js]
            ts = [
                jnp.dot(cb[xj, base + j], ws[(c >> 2) * 2 + (c & 1)], preferred_element_type=F32).astype(BF16)
                for j, c in zip(js, codes)
            ]
            ms = [jnp.dot(xs[(c >> 1) & 1, c >> 2], t, preferred_element_type=F32) for t, c in zip(ts, codes)]
            for j, m in zip(js, ms):
                scr[0, pl.ds(j, S, stride=PITCH), :] = m[:, :BLK]
                scr[1, pl.ds(j, S, stride=PITCH), :] = m[:, BLK:]
            return carry

        lax.fori_loop(0, HALF // batch, some, 0)

        def lay(g, carry):
            for a in range(2):
                at = pl.multiple_of((a * (BLK // UNIT) + g) * (UNIT * PITCH), 8)
                for b in range(2):
                    for r in range(UNIT):
                        v = scr[b, pl.ds(at + r * PITCH, HALF), :]
                        mb[xj, g, a * 2 + b, pl.ds(base, HALF), r * BLK:(r + 1) * BLK] = v.astype(BF16)
            return carry

        lax.fori_loop(0, BLK // UNIT, lay, 0, unroll=2)

    def own_code(j):
        return col_block[j] * 4 + col_slots[0, j] * 2 + col_slots[1, j]

    def code_at(xj):
        return lambda j: lab_s[xj, xj * OWN + j]

    pairs = ((x, xm), (xp, x2))
    ready = set()

    def contract(s, n, places):
        lo, hi = units_of(s)
        g = [axes(s)[1][m] for m in places]
        for m in places:
            if (s, m) not in ready:
                ready.add((s, m))
                sh[s, m].wait_recv()
        left = jnp.concatenate(
            [
                (
                    rb[b, :, :, :, lo * STEP:hi * STEP] if s < 4 else rb[:, :, yy(b), :, lo * STEP:hi * STEP]
                ).reshape(128, (hi - lo) * STEP)
                for b in g
            ],
            axis=0,
        )
        right = jnp.concatenate(
            [
                jnp.concatenate([mb[xj, u].reshape(4 * OWN, STEP) for u in range(lo, hi)], axis=1)
                for xj in pairs[n]
            ],
            axis=0,
        )
        got = lax.dot_general(left, right, (((1,), (1,)), ((), ())), preferred_element_type=F32)
        for i, b in enumerate(g):
            part = got[i * 128:(i + 1) * 128]
            if s < 4:
                acc[n, b] += part.reshape(2, 4, TB, 256)
            else:
                acc[n, :, :, yy(b)] += part.reshape(4, 2, TB, 256)

    near, far = (0, 1, 2), (3,)
    for s in (0, 4, 1, 5, 2, 6, 3, 7):
        first(s)
    labels = [
        go(remote(lab.at[x], lab.at[x], lab_send.at[n], lab_recv.at[n], dev((x + n + 1) % 4, y, z, core)))
        for n in range(3)
    ]
    columns(0)
    columns(1)
    for c in loads:
        c.wait()
    acc[...] = jnp.zeros_like(acc)
    images(x, 0, own_code)
    images(x, 1, own_code)
    for s in (0, 4, 1, 5, 2, 6, 3, 7):
        second(s)
    for s in (0, 4, 1, 5, 2, 6, 3, 7):
        arrived(s)
        third(s)
    for c in labels:
        c.wait_recv()
    lab_copy = pltpu.make_async_copy(lab.at[:, 0, :], lab_s, local.at[5])
    lab_copy.start()
    columns_wait(0)
    columns_far()
    lab_copy.wait()
    images(xm, 0, code_at(xm))
    images(xp, 1, code_at(xp))
    for s in (0, 4):
        fourth(s)
    columns_wait(1)
    images(xm, 1, code_at(xm))
    images(xp, 0, code_at(xp))
    for s in (1, 5):
        fourth(s)
    for s in (0, 4, 1, 5):
        contract(s, 0, near)
    for s in (2, 6):
        fourth(s)
    for s in (2, 6):
        contract(s, 0, near)
    for s in (3, 7):
        fourth(s)
    for s in (3, 7):
        contract(s, 0, near)
    for s in (0, 4):
        last(s)
    columns_wait(2)
    images(x2, 0, code_at(x2))
    images(x2, 1, code_at(x2))
    for s in (0, 4, 1, 5):
        contract(s, 1, near)
    for s in (1, 5):
        last(s)
    for s in (2, 6, 3, 7):
        contract(s, 1, near)
    for s in (0, 4):
        contract(s, 0, far)
        contract(s, 1, far)
    for s in (2, 6):
        last(s)
    for s in (1, 5):
        contract(s, 0, far)
        contract(s, 1, far)
    for s in (3, 7):
        last(s)
    for s in (2, 6, 3, 7):
        contract(s, 0, far)
        contract(s, 1, far)

    code = rb[:, :, :, :, FLAT:WIDE].reshape(8 * 64, 128).astype(F32).astype(jnp.int32)
    place = lax.broadcasted_iota(jnp.int32, (1, 128), 1) // OWN
    chosen = (code & 3) == place
    col_code = lab[0, 0:1, :] + lab[1, 0:1, :] + lab[2, 0:1, :] + lab[3, 0:1, :]
    total = jnp.zeros((8 * 64, 128), F32)
    for n in range(2):
        for m in range(2):
            v = jnp.where(chosen, acc[n, :, :, :, :, m * 128:(m + 1) * 128].reshape(8 * 64, 128), 0.0)
            v = v + pltpu.roll(v, 64, 1)
            v = v + pltpu.roll(v, 32, 1)
            total = jnp.where(place == pairs[n][m], v, total)
    total = jnp.where((code >> 2) == (col_code >> 2), total, 0.0)
    osend[...] = total.reshape(8, 2, 2, TB, 128)

    spot = pl.ds(pl.multiple_of(y_lo * 128, 128), 128)
    keep = pltpu.make_async_copy(osend.at[row], out.at[:, x, :, :, spot], local.at[6])
    outs = []
    for n in range(1, 8):
        to = (row + n) % 8
        outs.append(go(remote(osend.at[to], out.at[:, x, :, :, spot], out_send.at[n - 1], out_recv.at[n - 1], (to, col))))
    keep.start()
    for c in outs:
        c.wait_recv()
    keep.wait()
    for c in sent:
        c.wait_send()


def per_device(
    row_constraints, row_block, row_slots, col_constraints, col_block, col_slots, primal_x, inverse_z
):
    any_spec = pl.BlockSpec(memory_space=pl.ANY)
    smem = pl.BlockSpec(memory_space=pltpu.SMEM)
    dma = pltpu.SemaphoreType.DMA
    out = pl.pallas_call(
        kernel,
        out_shape=jax.ShapeDtypeStruct((2, 4, 2, TB, 256), F32),
        in_specs=[smem] * 4 + [any_spec] * 4,
        out_specs=any_spec,
        scratch_shapes=[
            pltpu.VMEM((TB, BLK, BLK), BF16),
            pltpu.VMEM((4, 2, 4, TB, WIDE), BF16),
            pltpu.VMEM((4, OWN, BLK, BLK), BF16),
            pltpu.VMEM((4, 8, 128), jnp.int32),
            pltpu.SMEM((4, 128), jnp.int32),
            pltpu.VMEM((2, 16, S, BLK), BF16),
            pltpu.VMEM((32, BLK, S), BF16),
            pltpu.VMEM((4, BLK // UNIT, 4, OWN, STEP), BF16),
            pltpu.VMEM((2, S * PITCH, BLK), F32),
            pltpu.VMEM((2, 4, 2, 4, TB, 256), F32),
            pltpu.VMEM((8, 2, 2, TB, 128), F32),
            dma((8, 8)), dma((8, 8)),
            dma((8, 4)), dma((8, 4)),
            dma((6,)), dma((6,)),
            dma((3,)), dma((3,)),
            dma((7,)), dma((7,)),
            dma((7,)),
        ],
        compiler_params=pltpu.CompilerParams(
            collective_id=0, has_side_effects=True, vmem_limit_bytes=58 * 1024 * 1024
        ),
    )(
        row_block, row_slots.T, col_block, col_slots.T,
        row_constraints, col_constraints, primal_x, inverse_z.reshape(32, BLK, S),
    )
    return out.reshape(16, TB, 256)


def solution(mesh):
    placed = (
        P(("row", "col"), None, None),
        P(("row", "col")),
        P(("row", "col"), None),
        P(("col", "row"), None, None),
        P(("col", "row")),
        P(("col", "row"), None),
        P(),
        P(),
    )
    return jax.shard_map(
        per_device, mesh=mesh, in_specs=placed, out_specs=P(None, "row", "col"), check_vma=False
    )
```

```python
import jax
import jax.numpy as jnp
from jax import lax
from jax.experimental import pallas as pl
from jax.experimental.pallas import tpu as pltpu
from jax.sharding import PartitionSpec as P

TB = 16
BLK = 128
S = 256
FLAT = BLK * BLK
WIDE = FLAT + 128
OWN = 32
HALF = OWN // 2
UNIT = 8
STEP = UNIT * BLK
PARTS = (2, 3, 2, 1)
PITCH = 17
MESH = pl.DeviceIdType.MESH
F32 = jnp.float32
BF16 = jnp.bfloat16


def units_of(s):
    start = (s // 4) * (BLK // UNIT // 2) + sum(PARTS[: s % 4])
    return start, start + PARTS[s % 4]


def lanes_of(s):
    first, last = units_of(s)
    return first * STEP, (WIDE if s == 7 else last * STEP)


def kernel(
    row_block, row_slots, col_block, col_slots, rows_in, cols_in, x_in, w_in, out,
    raw, rb, cb, lab, lab_s, xs, ws, mb, scr, acc, osend,
    row_send, row_recv, sib_send, sib_recv, col_send, col_recv, lab_send, lab_recv,
    out_send, out_recv, local,
):
    row, col = lax.axis_index("row"), lax.axis_index("col")
    y_lo, x = row // 4, row % 4
    y_hi, z, core = col // 8, (col // 2) % 4, col % 2
    y = y_hi * 2 + y_lo

    def dev(x_, y_, z_, core_):
        return ((y_ % 2) * 4 + x_, (y_ // 2) * 8 + z_ * 2 + core_)

    def yy(y_):
        return (y_ % 2) * 2 + y_ // 2

    yp, ym, y2 = (y + 1) % 4, (y + 3) % 4, (y + 2) % 4
    zp, zm, z2 = (z + 1) % 4, (z + 3) % 4, (z + 2) % 4
    xp, xm, x2 = (x + 1) % 4, (x + 3) % 4, (x + 2) % 4
    sibling = dev(x, y, z, 1 - core)
    dev_y = (dev(x, yp, z, core), dev(x, ym, z, core))
    dev_z = (dev(x, y, zp, core), dev(x, y, zm, core))
    dev_x = (dev(xp, y, z, core), dev(xm, y, z, core))

    barrier = pltpu.get_barrier_semaphore()
    y_other = y_hi * 2 + 1 - y_lo
    y_far = (y_other + 2) % 4
    greet = [dev(x, y_far, z, core), *dev_z, sibling]
    greet += [((row + n) % 8, col) for n in range(1, 8)]
    for d in greet:
        pl.semaphore_signal(barrier, inc=1, device_id=d, device_id_type=MESH)

    raw_load = pltpu.make_async_copy(rows_in, raw, local.at[0])
    raw_load.start()
    loads = [
        pltpu.make_async_copy(cols_in, cb.at[x], local.at[1]),
        pltpu.make_async_copy(w_in, ws, local.at[2]),
        pltpu.make_async_copy(x_in.at[:, :, pl.ds(0, BLK)], xs.at[0], local.at[3]),
        pltpu.make_async_copy(x_in.at[:, :, pl.ds(BLK, BLK)], xs.at[1], local.at[4]),
    ]
    for c in loads:
        c.start()

    sub = lax.broadcasted_iota(jnp.int32, (TB, 128), 0)
    mark = jnp.zeros((TB, 128), jnp.int32)
    for i in range(TB):
        mark = jnp.where(sub == i, row_block[i] * 4 + row_slots[0, i] * 2 + row_slots[1, i], mark)
    rb[z, core, yy(y), :, FLAT:WIDE] = mark.astype(F32).astype(BF16)
    lane = lax.broadcasted_iota(jnp.int32, (8, 128), 1) - x * OWN
    mark = jnp.zeros((8, 128), jnp.int32)
    for j in range(OWN):
        mark = jnp.where(lane == j, col_block[j] * 4 + col_slots[0, j] * 2 + col_slots[1, j], mark)
    lab[x] = mark

    raw_load.wait()
    for r in range(0, BLK, TB):
        tile = jnp.swapaxes(raw[:, r:r + TB, :], 0, 1)
        for n in range(TB):
            rb[z, core, yy(y), :, (r + n) * BLK:(r + n + 1) * BLK] = tile[n]
    pl.semaphore_wait(barrier, len(greet))

    def remote(src, dst, send, recv, to):
        return pltpu.make_async_remote_copy(
            src_ref=src, dst_ref=dst, send_sem=send, recv_sem=recv, device_id=to, device_id_type=MESH
        )

    sent = []

    def go(c):
        c.start()
        sent.append(c)
        return c

    def move(s, n, ref, to):
        return go(remote(ref, ref, row_send.at[s, n], row_recv.at[s, n], to))

    def block(s, a, b, cut):
        u, v = (b, a) if s < 4 else (a, b)
        return rb.at[u, core, yy(v), :, cut[0]:cut[1]]

    def axes(s):
        return ((y, ym, yp, y2), (z, zm, zp, z2)) if s < 4 else ((z, zm, zp, z2), (y, ym, yp, y2))

    def ways(s):
        return (dev_y, dev_z) if s < 4 else (dev_z, dev_y)

    def group(s, b, part=pl.ds(0, 4)):
        lo, hi = lanes_of(s)
        return rb.at[b, core, part, :, lo:hi] if s < 4 else rb.at[part, core, yy(b), :, lo:hi]

    w1, w2, w3, w4, sh = {}, {}, {}, {}, {}

    def first(s):
        f, g = axes(s)
        ref = block(s, f[0], g[0], lanes_of(s))
        w1[s] = [move(s, n, ref, ways(s)[0][n]) for n in range(2)]

    def second(s):
        for c in w1[s]:
            c.wait_recv()
        f, g = axes(s)
        lo, hi = lanes_of(s)
        mid = lo + PARTS[s % 4] * STEP // 2
        cut = ((lo, mid), (mid, hi))
        w2[s] = [move(s, 2 + n, block(s, f[1 + n], g[0], cut[n]), ways(s)[0][n]) for n in range(2)]

    def arrived(s):
        for c in w2[s]:
            c.wait_recv()
        share(s, 0)

    def third(s):
        ref = group(s, axes(s)[1][0])
        w3[s] = [move(s, 4 + n, ref, ways(s)[1][n]) for n in range(2)]

    def fourth(s):
        for c in w3[s]:
            c.wait_recv()
        f, g = axes(s)
        w4[s] = [move(s, 6 + n, group(s, g[1 + n], pl.ds(2 * n, 2)), ways(s)[1][n]) for n in range(2)]
        share(s, 1)
        share(s, 2)

    def last(s):
        for c in w4[s]:
            c.wait_recv()
        share(s, 3)

    def share(s, m):
        ref = group(s, axes(s)[1][m])
        sh[s, m] = go(remote(ref, ref, sib_send.at[s, m], sib_recv.at[s, m], sibling))

    c1 = {}

    def columns(h):
        for n in range(2):
            part = pl.ds((HALF * h) if n == 0 else (HALF * (1 - h)), HALF)
            c1[h, n] = go(remote(cols_in.at[part], cb.at[x, part], col_send.at[2 * h + n], col_recv.at[2 * h + n], dev_x[n]))

    def columns_far():
        for n in range(2):
            ref = cb.at[(xm, xp)[n], pl.ds(HALF * n, HALF)]
            c1[2, n] = go(remote(ref, ref, col_send.at[4 + n], col_recv.at[4 + n], dev_x[n]))

    def columns_wait(h):
        for n in range(2):
            c1[h, n].wait_recv()

    def images(xj, h, code_of):
        base = h * HALF
        batch = 16

        def some(i, carry):
            js = [i * batch + n for n in range(batch)]
            codes = [code_of(base + j) for j in js]
            ts = [
                jnp.dot(cb[xj, base + j], ws[(c >> 2) * 2 + (c & 1)], preferred_element_type=F32).astype(BF16)
                for j, c in zip(js, codes)
            ]
            ms = [jnp.dot(xs[(c >> 1) & 1, c >> 2], t, preferred_element_type=F32) for t, c in zip(ts, codes)]
            for j, m in zip(js, ms):
                scr[0, pl.ds(j, S, stride=PITCH), :] = m[:, :BLK]
                scr[1, pl.ds(j, S, stride=PITCH), :] = m[:, BLK:]
            return carry

        lax.fori_loop(0, HALF // batch, some, 0)

        def lay(g, carry):
            for a in range(2):
                at = pl.multiple_of((a * (BLK // UNIT) + g) * (UNIT * PITCH), 8)
                for b in range(2):
                    for r in range(UNIT):
                        v = scr[b, pl.ds(at + r * PITCH, HALF), :]
                        mb[xj, g, a * 2 + b, pl.ds(base, HALF), r * BLK:(r + 1) * BLK] = v.astype(BF16)
            return carry

        lax.fori_loop(0, BLK // UNIT, lay, 0, unroll=2)

    def own_code(j):
        return col_block[j] * 4 + col_slots[0, j] * 2 + col_slots[1, j]

    def code_at(xj):
        return lambda j: lab_s[xj, xj * OWN + j]

    pairs = ((x, xm), (xp, x2))
    ready = set()

    def contract(s, n, places):
        lo, hi = units_of(s)
        g = [axes(s)[1][m] for m in places]
        for m in places:
            if (s, m) not in ready:
                ready.add((s, m))
                sh[s, m].wait_recv()
        left = jnp.concatenate(
            [
                (
                    rb[b, :, :, :, lo * STEP:hi * STEP] if s < 4 else rb[:, :, yy(b), :, lo * STEP:hi * STEP]
                ).reshape(128, (hi - lo) * STEP)
                for b in g
            ],
            axis=0,
        )
        right = jnp.concatenate(
            [
                jnp.concatenate([mb[xj, u].reshape(4 * OWN, STEP) for u in range(lo, hi)], axis=1)
                for xj in pairs[n]
            ],
            axis=0,
        )
        got = lax.dot_general(left, right, (((1,), (1,)), ((), ())), preferred_element_type=F32)
        for i, b in enumerate(g):
            part = got[i * 128:(i + 1) * 128]
            if s < 4:
                acc[n, b] += part.reshape(2, 4, TB, 256)
            else:
                acc[n, :, :, yy(b)] += part.reshape(4, 2, TB, 256)

    near, far = (0, 1, 2), (3,)
    for s in (0, 4, 1, 5, 2, 6, 3, 7):
        first(s)
    labels = [
        go(remote(lab.at[x], lab.at[x], lab_send.at[n], lab_recv.at[n], dev((x + n + 1) % 4, y, z, core)))
        for n in range(3)
    ]
    columns(0)
    columns(1)
    for c in loads:
        c.wait()
    acc[...] = jnp.zeros_like(acc)
    images(x, 0, own_code)
    images(x, 1, own_code)
    for s in (0, 4, 1, 5, 2, 6, 3, 7):
        second(s)
    for s in (0, 4, 1, 5, 2, 6, 3, 7):
        arrived(s)
        third(s)
    for c in labels:
        c.wait_recv()
    lab_copy = pltpu.make_async_copy(lab.at[:, 0, :], lab_s, local.at[5])
    lab_copy.start()
    columns_wait(0)
    columns_far()
    lab_copy.wait()
    images(xm, 0, code_at(xm))
    images(xp, 1, code_at(xp))
    for s in (0, 4):
        fourth(s)
    columns_wait(1)
    images(xm, 1, code_at(xm))
    images(xp, 0, code_at(xp))
    for s in (1, 5):
        fourth(s)
    for s in (0, 4, 1, 5):
        contract(s, 0, near)
    for s in (2, 6):
        fourth(s)
    for s in (2, 6):
        contract(s, 0, near)
    for s in (3, 7):
        fourth(s)
    for s in (3, 7):
        contract(s, 0, near)
    for s in (0, 4):
        last(s)
    columns_wait(2)
    images(x2, 0, code_at(x2))
    images(x2, 1, code_at(x2))
    for s in (0, 4, 1, 5):
        contract(s, 1, near)
    for s in (1, 5):
        last(s)
    for s in (2, 6, 3, 7):
        contract(s, 1, near)
    for s in (0, 4):
        contract(s, 0, far)
        contract(s, 1, far)
    for s in (2, 6):
        last(s)
    for s in (1, 5):
        contract(s, 0, far)
        contract(s, 1, far)
    for s in (3, 7):
        last(s)
    for s in (2, 6, 3, 7):
        contract(s, 0, far)
        contract(s, 1, far)

    code = rb[:, :, :, :, FLAT:WIDE].reshape(8 * 64, 128).astype(F32).astype(jnp.int32)
    place = lax.broadcasted_iota(jnp.int32, (1, 128), 1) // OWN
    chosen = (code & 3) == place
    col_code = lab[0, 0:1, :] + lab[1, 0:1, :] + lab[2, 0:1, :] + lab[3, 0:1, :]
    total = jnp.zeros((8 * 64, 128), F32)
    for n in range(2):
        for m in range(2):
            v = jnp.where(chosen, acc[n, :, :, :, :, m * 128:(m + 1) * 128].reshape(8 * 64, 128), 0.0)
            v = v + pltpu.roll(v, 64, 1)
            v = v + pltpu.roll(v, 32, 1)
            total = jnp.where(place == pairs[n][m], v, total)
    total = jnp.where((code >> 2) == (col_code >> 2), total, 0.0)
    osend[...] = total.reshape(8, 2, 2, TB, 128)

    spot = pl.ds(pl.multiple_of(y_lo * 128, 128), 128)
    keep = pltpu.make_async_copy(osend.at[row], out.at[:, x, :, :, spot], local.at[6])
    outs = []
    for n in range(1, 8):
        to = (row + n) % 8
        outs.append(go(remote(osend.at[to], out.at[:, x, :, :, spot], out_send.at[n - 1], out_recv.at[n - 1], (to, col))))
    keep.start()
    for c in outs:
        c.wait_recv()
    keep.wait()
    for c in sent:
        c.wait_send()


def per_device(
    row_constraints, row_block, row_slots, col_constraints, col_block, col_slots, primal_x, inverse_z
):
    any_spec = pl.BlockSpec(memory_space=pl.ANY)
    smem = pl.BlockSpec(memory_space=pltpu.SMEM)
    dma = pltpu.SemaphoreType.DMA
    out = pl.pallas_call(
        kernel,
        out_shape=jax.ShapeDtypeStruct((2, 4, 2, TB, 256), F32),
        in_specs=[smem] * 4 + [any_spec] * 4,
        out_specs=any_spec,
        scratch_shapes=[
            pltpu.VMEM((TB, BLK, BLK), BF16),
            pltpu.VMEM((4, 2, 4, TB, WIDE), BF16),
            pltpu.VMEM((4, OWN, BLK, BLK), BF16),
            pltpu.VMEM((4, 8, 128), jnp.int32),
            pltpu.SMEM((4, 128), jnp.int32),
            pltpu.VMEM((2, 16, S, BLK), BF16),
            pltpu.VMEM((32, BLK, S), BF16),
            pltpu.VMEM((4, BLK // UNIT, 4, OWN, STEP), BF16),
            pltpu.VMEM((2, S * PITCH, BLK), F32),
            pltpu.VMEM((2, 4, 2, 4, TB, 256), F32),
            pltpu.VMEM((8, 2, 2, TB, 128), F32),
            dma((8, 8)), dma((8, 8)),
            dma((8, 4)), dma((8, 4)),
            dma((6,)), dma((6,)),
            dma((3,)), dma((3,)),
            dma((7,)), dma((7,)),
            dma((7,)),
        ],
        compiler_params=pltpu.CompilerParams(
            collective_id=0, has_side_effects=True, vmem_limit_bytes=58 * 1024 * 1024
        ),
    )(
        row_block, row_slots.T, col_block, col_slots.T,
        row_constraints, col_constraints, primal_x, inverse_z.reshape(32, BLK, S),
    )
    return out.reshape(16, TB, 256)


def solution(mesh):
    placed = (
        P(("row", "col"), None, None),
        P(("row", "col")),
        P(("row", "col"), None),
        P(("col", "row"), None, None),
        P(("col", "row")),
        P(("col", "row"), None),
        P(),
        P(),
    )
    return jax.shard_map(
        per_device, mesh=mesh, in_specs=placed, out_specs=P(None, "row", "col"), check_vma=False
    )
```
